32 devices in a mesh: wide: 16 (over z, y, core), narrow: 2 (over x).
Axes of the slice: x: 2, y: 2, z: 4, core: 2. Of those that a mesh axis runs over, the one named last changes fastest.
Arguments:
- right_side: float32 [96, 128, 256], P(('wide', 'narrow')), may hold values from -6 to 6
- diag_inverse: float32 [96, 128, 128], P(('wide', 'narrow')), may hold values from -1 to 1, as said below
- off_tiles: float32 [96, 48, 128, 128], P('wide', 'narrow'), may hold values from -0.078125 to 0.078125
- tile_columns: int32 [96, 48], P('wide', 'narrow'), may hold values from 0 to 95, as said below
- colors: int32 [96], replicated, may hold values from 0 to 2, as said below
Outputs:
- potentials: float32 [96, 128, 256], P(('wide', 'narrow'))
The draws below stay inside these ranges and needn't reach their ends.
Inputs may be any that keep to these rules, and one draw needn't show every extreme that they name: `colors`: each device along wide+narrow owns 3 consecutive blocks, exactly 1 of each color. `tile_columns`: slot k of a block row names a block owned by a device whose narrow index is k // 24, and of another color than the row's block. `diag_inverse`: symmetric tiles.
All inputs are finite; a program needn't handle non-finite values.
Results may differ from the reference program's by a relative error of at most 0.0001.
Values sent between devices are 32-bit elements; how exact they have to be, the bound alone decides.
A program may use at most 128 MiB of HBM per device.

```python
import jax
import jax.numpy as jnp
from jax import lax

TILE = 128
LABELS = 256
K = 48
CB = 1
OB = 3
KD = 24
NB = 96
N_WIDE = 16
N_NARROW = 2


def color_table(key):
    group_count = NB // OB
    group_keys = jax.random.split(key, group_count)
    pattern = jnp.arange(OB, dtype=jnp.int32) // CB
    table = jax.vmap(lambda one_key: jax.random.permutation(one_key, pattern))(group_keys)
    return table.reshape(NB).astype(jnp.int32)


def draw_colors(key, part):
    return color_table(jax.random.fold_in(key, 11))


def draw_tile_columns(key, part):
    block_hue = color_table(jax.random.fold_in(key, 11))
    table = block_hue.reshape(NB // OB, OB)
    owner_sorted = jnp.argsort(table, axis=1, stable=True).astype(jnp.int32)
    first_key, second_key, third_key = jax.random.split(jax.random.fold_in(key, 23), 3)
    owner_wide = jax.random.randint(first_key, (NB, K), 0, N_WIDE).astype(jnp.int32)
    offset = jax.random.randint(second_key, (NB, K), 1, 3).astype(jnp.int32)
    other_hue = (block_hue[:, None] + offset) % 3
    rank_pick = jax.random.randint(third_key, (NB, K), 0, CB).astype(jnp.int32)
    slot_group = jnp.arange(K, dtype=jnp.int32) // KD
    owner = owner_wide * N_NARROW + slot_group[None, :]
    local_row = owner_sorted[owner, other_hue * CB + rank_pick]
    return (owner * OB + local_row).astype(jnp.int32)


def draw_diag_inverse(key, part):
    first_key, second_key = jax.random.split(key)
    noise = jax.random.normal(first_key, (NB, TILE, TILE), jnp.float32)
    noise = jnp.clip(noise, -2.5, 2.5) * (0.3 / TILE ** 0.5)
    symmetric = (noise + jnp.swapaxes(noise, 1, 2)) * 0.70710678
    diagonal = 0.35 + 0.35 * jax.random.uniform(second_key, (NB, TILE), jnp.float32)
    return symmetric + diagonal[:, :, None] * jnp.eye(TILE, dtype=jnp.float32)[None, :, :]


def levels(own_key, dims, cuts, least, largest):
    def one(axis_at, parts):
        steps = jax.random.uniform(jax.random.fold_in(jax.random.fold_in(own_key, 6), axis_at), (parts,), jnp.float32, least / len(cuts), largest / len(cuts))
        return jnp.repeat(jnp.exp(steps), dims[axis_at] // parts).reshape((-1,) + (1,) * (len(dims) - axis_at - 1))

    level = one(*cuts[0])
    for cut in cuts[1:]:
        level = level * one(*cut)
    return level


def scatter_about(stream_key, extent, spread, limit, pieces=(), kind=jnp.bfloat16):
    loudness = levels(stream_key, extent, pieces, -0.22, 0.18) if pieces else 1.0
    drawn = jax.random.normal(stream_key, extent, jnp.float32) * spread * loudness
    return jnp.minimum(jnp.maximum(drawn, -limit), limit).astype(kind)


def setup_inputs(seed: int = 0) -> dict:
    streams_of = jax.random.split(jax.random.key(seed), 6)
    return {
        "right_side": scatter_about(streams_of[0], (NB, TILE, LABELS), 1.0, 6.0, ((0, 32),), jnp.float32),
        "diag_inverse": draw_diag_inverse(jax.random.fold_in(streams_of[5], 71), 0),
        "off_tiles": scatter_about(streams_of[2], (NB, K, TILE, TILE), (TILE * K) ** -0.5, 0.078125, ((0, 16), (1, 2)), jnp.float32),
        "tile_columns": draw_tile_columns(jax.random.fold_in(streams_of[5], 71), 0),
        "colors": draw_colors(jax.random.fold_in(streams_of[5], 71), 0),
    }


def one_row(potential, off_tiles, tile_columns, row_id):
    picked = potential[tile_columns[row_id]]
    return jnp.einsum("kab,kbl->al", off_tiles[row_id], picked, precision=lax.Precision.HIGHEST)


def reference(right_side, diag_inverse, off_tiles, tile_columns, colors):
    color_order = jnp.argsort(colors, stable=True).astype(jnp.int32)
    per_color = NB // 3
    potential = jnp.zeros(right_side.shape, jnp.float32)
    for section, color_now in enumerate((0, 1, 2, 1, 0)):
        row_ids = color_order[color_now * per_color:(color_now + 1) * per_color]
        source = right_side[row_ids]
        if section > 0:
            neighbour = lax.map(lambda row_id: one_row(potential, off_tiles, tile_columns, row_id), row_ids)
            source = source - neighbour
        updated = jnp.einsum("rab,rbl->ral", diag_inverse[row_ids], source, precision=lax.Precision.HIGHEST)
        potential = potential.at[row_ids].set(updated)
    return potential
```

```python
import functools

import jax
import jax.numpy as jnp
from jax import lax
from jax.experimental import pallas as pl
from jax.experimental.pallas import tpu as pltpu
from jax.sharding import PartitionSpec as P

MESH = pl.DeviceIdType.MESH
HALF = 128


def split(value):
    high = value.astype(jnp.bfloat16)
    low = (value - high.astype(jnp.float32)).astype(jnp.bfloat16)
    return high, low


def fold(wide_sum):
    t = wide_sum.shape[0] // 2
    return (wide_sum[:t, :HALF] + wide_sum[:t, HALF:]) + (wide_sum[t:, :HALF] + wide_sum[t:, HALF:])


def kernel(
    n_wide, n_narrow, colors, columns, side_ref, diag_ref, tiles_ref, out_ref,
    stage, ta, da, vb, gathered, psend, precv, xout, index, acc, own_sum,
    load_sem, ring_send, ring_recv, sib_send, sib_recv, part_send, part_recv,
):
    wide = lax.axis_index("wide")
    narrow = lax.axis_index("narrow")
    rows, kd = stage.shape[0], stage.shape[1]
    pairs = kd // 2
    chips = n_wide // 2
    depth = chips // 2
    zs = chips // 2
    chip, core = lax.div(wide, 2), lax.rem(wide, 2)
    z, y = lax.div(chip, 2), lax.rem(chip, 2)
    here = z + y * (2 * zs - 1 - 2 * z)

    def at(position, which):
        q = lax.rem(position + 2 * chips, chips)
        qy = lax.div(q, zs)
        qz = q + qy * (2 * zs - 1 - 2 * q)
        return (qz * 2 + qy) * 2 + which

    right, left, sibling = at(here + 1, core), at(here - 1, core), at(here, 1 - core)

    for r in range(rows):
        pltpu.make_async_copy(tiles_ref.at[r], stage.at[r], load_sem.at[r]).start()

    for h in range(2):
        @pl.loop(0, 3 * n_wide)
        def _(i):
            vb[h, i] = jnp.zeros(vb.shape[2:], jnp.bfloat16)

    def pick(color, owner_narrow):
        base = (wide * n_narrow + owner_narrow) * 3
        return jnp.where(colors[base + 1] == color, 1, jnp.where(colors[base + 2] == color, 2, 0))

    barrier = pltpu.get_barrier_semaphore()
    for peer in (right, left, sibling):
        pl.semaphore_signal(barrier, inc=1, device_id=(peer, narrow), device_id_type=MESH)
    for d in range(1, n_narrow):
        peer = lax.rem(narrow + d, n_narrow)
        pl.semaphore_signal(barrier, inc=1, device_id=(wide, peer), device_id_type=MESH)
    pl.semaphore_wait(barrier, 3 + n_narrow - 1)

    def ring_copy(s, h, origin, rel, target):
        ref = gathered.at[s, h, origin]
        return pltpu.make_async_remote_copy(
            src_ref=ref, dst_ref=ref, send_sem=ring_send.at[s, h, rel], recv_sem=ring_recv.at[s, h, rel],
            device_id=(target, narrow), device_id_type=MESH,
        )

    def sib_copy(s, h, origin, rel):
        ref = gathered.at[s, h, origin]
        return pltpu.make_async_remote_copy(
            src_ref=ref, dst_ref=ref, send_sem=sib_send.at[s, h, rel], recv_sem=sib_recv.at[s, h, rel],
            device_id=(sibling, narrow), device_id_type=MESH,
        )

    def part_copy(s, h, d):
        target = lax.rem(narrow + d, n_narrow)
        return pltpu.make_async_remote_copy(
            src_ref=psend.at[s, h, d - 1], dst_ref=precv.at[s, h, d - 1],
            send_sem=part_send.at[s, h, d - 1], recv_sem=part_recv.at[s, h, d - 1],
            device_id=(wide, target), device_id_type=MESH,
        )

    def color_of(s):
        return s - 2 * jnp.maximum(s - 2, 0)

    def keep(s, h, origin):
        high, low = split(gathered[s, h, origin])
        spot = color_of(s) * n_wide + origin
        vb[h, spot, :, 0:HALF] = high
        vb[h, spot, :, HALF:] = low

    def reach(h):
        return (depth, depth - 1) if h == 0 else (depth - 1, depth)

    def start_gather(s, h):
        ring_copy(s, h, wide, 1, right).start()
        ring_copy(s, h, wide, chips - 1, left).start()
        sib_copy(s, h, wide, 0).start()
        keep(s, h, wide)

    def arrivals(h, j):
        if j == 0:
            return [0]
        r, l = reach(h)
        return ([j] if j <= r else []) + ([chips - j] if j <= l else [])

    def take_sibling(s, h, j):
        for rel in arrivals(h, j):
            origin = at(here - rel, 1 - core)
            sib_copy(s, h, origin, rel).wait_recv()
            keep(s, h, origin)

    def relay(s, h, j):
        r, l = reach(h)
        for rel in arrivals(h, j):
            origin = at(here - rel, core)
            rightward = rel == j and j <= r
            ring_copy(s, h, origin, rel, right if rightward else left).wait_recv()
            if rightward and j < r:
                ring_copy(s, h, origin, rel + 1, right).start()
            if not rightward and j < l:
                ring_copy(s, h, origin, rel - 1, left).start()
            sib_copy(s, h, origin, rel).start()
        for rel in arrivals(h, j):
            keep(s, h, at(here - rel, core))
        take_sibling(s, h, j - 1)

    def solve(s, h, side):
        color = color_of(s)
        high, low = split(side)
        rhs = jnp.concatenate([high, low], axis=1)
        return fold(jnp.dot(da[color], rhs, preferred_element_type=jnp.float32))

    def columns_of(h):
        return slice(h * HALF, (h + 1) * HALF)

    for color in range(3):
        high, low = split(diag_ref[pick(color, narrow)])
        t = high.shape[0]
        da[color, 0:t] = high
        da[color, t:] = low

    for h in range(2):
        gathered[0, h, wide] = solve(0, h, side_ref[pick(0, narrow), :, columns_of(h)])
        start_gather(0, h)

    for color in range(3):
        @pl.loop(0, n_narrow)
        def _(n):
            row = n * 3 + pick(color, n)

            @pl.loop(0, kd)
            def _(k):
                column = columns[row, k]
                index[(color * n_narrow + n) * kd + k] = colors[column] * n_wide + lax.div(column, 3 * n_narrow)

    for r in range(rows):
        pltpu.make_async_copy(tiles_ref.at[r], stage.at[r], load_sem.at[r]).wait()

    done = 0
    for turn, color in enumerate((1, 2, 0)):
        @pl.loop(0, n_narrow)
        def _(n):
            row = n * 3 + pick(color, n)
            t = stage.shape[2]

            @pl.loop(0, kd // 2)
            def _(k):
                for part in range(2):
                    high, low = split(stage[row, 2 * k + part])
                    ta[color * n_narrow + n, k, 0:t, part * t:(part + 1) * t] = high
                    ta[color * n_narrow + n, k, t:, part * t:(part + 1) * t] = low

        while done < depth * (turn + 1) // 3:
            done += 1
            relay(0, 0, done)
            if done > 1:
                relay(0, 1, done - 1)

    cuts = max(1, min(pairs, depth // n_narrow))
    pieces = cuts * n_narrow

    def section(s, h, step, first, last):
        color = color_of(s)
        take_sibling(s - 1, h, depth)
        count, at_step = 0, first
        for d in list(range(1, n_narrow)) + [0]:
            target = lax.rem(narrow + d, n_narrow)
            group = color * n_narrow + target
            for cut in range(cuts):
                total = None
                for k in range(cut * pairs // cuts, (cut + 1) * pairs // cuts):
                    spot = group * kd + 2 * k
                    rhs = jnp.concatenate([vb[h, index[spot]], vb[h, index[spot + 1]]], axis=0)
                    term = jnp.dot(ta[group, k], rhs, preferred_element_type=jnp.float32)
                    total = term if total is None else total + term
                if cut == 0:
                    acc[...] = fold(total)
                else:
                    acc[...] += fold(total)
                if cut == cuts - 1:
                    if d > 0:
                        psend[s - 1, h, d - 1] = acc[...]
                        part_copy(s - 1, h, d).start()
                    else:
                        own_sum[...] = acc[...]
                count += 1
                while at_step <= last and (at_step - first) < (last - first + 1) * count // pieces:
                    step(at_step)
                    at_step += 1
        summed = own_sum[...]
        for d in range(1, n_narrow):
            part_copy(s - 1, h, d).wait_recv()
            summed = summed + precv[s - 1, h, d - 1]
        x = solve(s, h, side_ref[pick(color, narrow), :, columns_of(h)] - summed)
        xout[color, :, columns_of(h)] = x

        @pl.when(s < 4)
        def _():
            gathered[s, h, wide] = x
            start_gather(s, h)

    def both(s, carry):
        def step_one(j):
            relay(s - 1, 1, j)

        def step_zero(j):
            @pl.when(s < 4)
            def _():
                relay(s, 0, j)

        @pl.when(s == 1)
        def _():
            relay(0, 1, depth)

        @pl.when(s > 1)
        def _():
            relay(s - 1, 1, 1)

        section_zero(s, step_one)
        section(s, 1, step_zero, 1, depth)
        return carry

    def section_zero(s, step_one):
        def guarded(j):
            @pl.when(s > 1)
            def _():
                step_one(j)

        section(s, 0, guarded, 2, depth)

    lax.fori_loop(1, 5, both, 0)

    for j in range(3):
        out_ref[j] = xout[colors[(wide * n_narrow + narrow) * 3 + j]]

    @pl.loop(0, 4)
    def _(s):
        for h in range(2):
            @pl.loop(0, chips)
            def _(rel):
                sib_copy(s, h, wide, rel).wait_send()

            @pl.loop(1, chips)
            def _(rel):
                ring_copy(s, h, wide, rel, right).wait_send()

            for d in range(1, n_narrow):
                part_copy(s, h, d).wait_send()


def shards(n_wide, n_narrow, right_side, diag_inverse, off_tiles, tile_columns, colors):
    own, tile, labels = right_side.shape
    rows, kd = off_tiles.shape[:2]
    chips = n_wide // 2
    others = n_narrow - 1
    f32, b16 = jnp.float32, jnp.bfloat16
    dma = pltpu.SemaphoreType.DMA
    vmem = pl.BlockSpec(memory_space=pltpu.VMEM)
    smem = pl.BlockSpec(memory_space=pltpu.SMEM)
    return pl.pallas_call(
        functools.partial(kernel, n_wide, n_narrow),
        out_shape=jax.ShapeDtypeStruct((own, tile, labels), f32),
        in_specs=[smem, smem, vmem, vmem, pl.BlockSpec(memory_space=pl.ANY)],
        out_specs=vmem,
        scratch_shapes=[
            pltpu.VMEM((rows, kd, tile, tile), f32),
            pltpu.VMEM((rows, kd // 2, 2 * tile, 2 * tile), b16),
            pltpu.VMEM((3, 2 * tile, tile), b16),
            pltpu.VMEM((2, 3 * n_wide, tile, 2 * HALF), b16),
            pltpu.VMEM((4, 2, n_wide, tile, HALF), f32),
            pltpu.VMEM((4, 2, others, tile, HALF), f32),
            pltpu.VMEM((4, 2, others, tile, HALF), f32),
            pltpu.VMEM((3, tile, labels), f32),
            pltpu.SMEM((rows * kd,), jnp.int32),
            pltpu.VMEM((tile, HALF), f32),
            pltpu.VMEM((tile, HALF), f32),
            dma((rows,)),
            dma((4, 2, chips)),
            dma((4, 2, chips)),
            dma((4, 2, chips)),
            dma((4, 2, chips)),
            dma((4, 2, others)),
            dma((4, 2, others)),
        ],
        compiler_params=pltpu.CompilerParams(
            collective_id=0, has_side_effects=True, vmem_limit_bytes=63 * 1024 * 1024
        ),
        cost_estimate=pl.CostEstimate(flops=8 * 10**9, bytes_accessed=10**7, transcendentals=0),
    )(colors, tile_columns, right_side, diag_inverse, off_tiles)


def solution(mesh):
    return jax.shard_map(
        functools.partial(shards, mesh.shape["wide"], mesh.shape["narrow"]),
        mesh=mesh,
        in_specs=(
            P(("wide", "narrow"), None, None),
            P(("wide", "narrow"), None, None),
            P("wide", "narrow", None, None),
            P("wide", "narrow"),
            P(),
        ),
        out_specs=P(("wide", "narrow"), None, None),
        check_vma=False,
    )
```

```python
import functools

import jax
import jax.numpy as jnp
from jax import lax
from jax.experimental import pallas as pl
from jax.experimental.pallas import tpu as pltpu
from jax.sharding import PartitionSpec as P

MESH = pl.DeviceIdType.MESH
HALF = 128


def split(value):
    high = value.astype(jnp.bfloat16)
    low = (value - high.astype(jnp.float32)).astype(jnp.bfloat16)
    return high, low


def fold(wide_sum):
    t = wide_sum.shape[0] // 2
    return (wide_sum[:t, :HALF] + wide_sum[:t, HALF:]) + (wide_sum[t:, :HALF] + wide_sum[t:, HALF:])


def kernel(
    n_wide, n_narrow, colors, columns, side_ref, diag_ref, tiles_ref, out_ref,
    stage, ta, da, vb, gathered, psend, precv, xout, index, acc, own_sum,
    load_sem, ring_send, ring_recv, sib_send, sib_recv, part_send, part_recv,
):
    wide = lax.axis_index("wide")
    narrow = lax.axis_index("narrow")
    rows, kd = stage.shape[0], stage.shape[1]
    pairs = kd // 2
    chips = n_wide // 2
    zs = chips // 2
    chip, core = lax.div(wide, 2), lax.rem(wide, 2)
    z, y = lax.div(chip, 2), lax.rem(chip, 2)

    def at(at_z, at_y, which):
        return (lax.rem(at_z + zs, zs) * 2 + at_y) * 2 + which

    across, sibling = at(z, 1 - y, core), at(z, y, 1 - core)
    steps = sorted(range(1, zs), key=lambda d: min(d, zs - d))

    for r in range(rows):
        pltpu.make_async_copy(tiles_ref.at[r], stage.at[r], load_sem.at[r]).start()

    for h in range(2):
        @pl.loop(0, 3 * n_wide)
        def _(i):
            vb[h, i] = jnp.zeros(vb.shape[2:], jnp.bfloat16)

    def pick(color, owner_narrow):
        base = (wide * n_narrow + owner_narrow) * 3
        return jnp.where(colors[base + 1] == color, 1, jnp.where(colors[base + 2] == color, 2, 0))

    barrier = pltpu.get_barrier_semaphore()
    for peer in [across, sibling] + [at(z + d, y, core) for d in steps]:
        pl.semaphore_signal(barrier, inc=1, device_id=(peer, narrow), device_id_type=MESH)
    for d in range(1, n_narrow):
        peer = lax.rem(narrow + d, n_narrow)
        pl.semaphore_signal(barrier, inc=1, device_id=(wide, peer), device_id_type=MESH)
    pl.semaphore_wait(barrier, 1 + zs + n_narrow - 1)

    def ring_copy(s, h, origin, rel, target):
        ref = gathered.at[s, h, origin]
        return pltpu.make_async_remote_copy(
            src_ref=ref, dst_ref=ref, send_sem=ring_send.at[s, h, rel], recv_sem=ring_recv.at[s, h, rel],
            device_id=(target, narrow), device_id_type=MESH,
        )

    def sib_copy(s, h, origin, rel):
        ref = gathered.at[s, h, origin]
        return pltpu.make_async_remote_copy(
            src_ref=ref, dst_ref=ref, send_sem=sib_send.at[s, h, rel], recv_sem=sib_recv.at[s, h, rel],
            device_id=(sibling, narrow), device_id_type=MESH,
        )

    def part_copy(s, h, d):
        target = lax.rem(narrow + d, n_narrow)
        return pltpu.make_async_remote_copy(
            src_ref=psend.at[s, h, d - 1], dst_ref=precv.at[s, h, d - 1],
            send_sem=part_send.at[s, h, d - 1], recv_sem=part_recv.at[s, h, d - 1],
            device_id=(wide, target), device_id_type=MESH,
        )

    def color_of(s):
        return s - 2 * jnp.maximum(s - 2, 0)

    def keep(s, h, origin):
        high, low = split(gathered[s, h, origin])
        spot = color_of(s) * n_wide + origin
        vb[h, spot, :, 0:HALF] = high
        vb[h, spot, :, HALF:] = low

    def start_gather(s, h):
        ring_copy(s, h, wide, zs, across).start()
        for d in steps:
            ring_copy(s, h, wide, d, at(z + d, y, core)).start()
        sib_copy(s, h, wide, 0).start()
        keep(s, h, wide)

    def middle(s, h):
        for d in steps:
            origin = at(z - d, y, core)
            ring_copy(s, h, origin, d, across).wait_recv()
            ring_copy(s, h, origin, zs + d, across).start()
            sib_copy(s, h, origin, d).start()
        for d in steps:
            keep(s, h, at(z - d, y, core))

    def finish(s, h):
        for d in [0] + steps:
            origin = at(z - d, 1 - y, core)
            ring_copy(s, h, origin, zs + d, across).wait_recv()
            sib_copy(s, h, origin, zs + d).start()
            keep(s, h, origin)
        for column in range(2):
            for d in [0] + steps:
                origin = at(z - d, y + column * (1 - 2 * y), 1 - core)
                sib_copy(s, h, origin, column * zs + d).wait_recv()
                keep(s, h, origin)

    def solve(s, h, side):
        color = color_of(s)
        high, low = split(side)
        rhs = jnp.concatenate([high, low], axis=1)
        return fold(jnp.dot(da[color], rhs, preferred_element_type=jnp.float32))

    def columns_of(h):
        return slice(h * HALF, (h + 1) * HALF)

    for color in range(3):
        high, low = split(diag_ref[pick(color, narrow)])
        t = high.shape[0]
        da[color, 0:t] = high
        da[color, t:] = low

    for h in range(2):
        gathered[0, h, wide] = solve(0, h, side_ref[pick(0, narrow), :, columns_of(h)])
        start_gather(0, h)

    for color in range(3):
        @pl.loop(0, n_narrow)
        def _(n):
            row = n * 3 + pick(color, n)

            @pl.loop(0, kd)
            def _(k):
                column = columns[row, k]
                index[(color * n_narrow + n) * kd + k] = colors[column] * n_wide + lax.div(column, 3 * n_narrow)

    for r in range(rows):
        pltpu.make_async_copy(tiles_ref.at[r], stage.at[r], load_sem.at[r]).wait()

    for turn, color in enumerate((1, 2, 0)):
        @pl.loop(0, n_narrow)
        def _(n):
            row = n * 3 + pick(color, n)
            t = stage.shape[2]

            @pl.loop(0, kd // 2)
            def _(k):
                for part in range(2):
                    high, low = split(stage[row, 2 * k + part])
                    ta[color * n_narrow + n, k, 0:t, part * t:(part + 1) * t] = high
                    ta[color * n_narrow + n, k, t:, part * t:(part + 1) * t] = low

        if turn < 2:
            middle(0, turn)

    cuts = 2 if pairs % 2 == 0 else 1

    def section(s, h, step):
        color = color_of(s)
        finish(s - 1, h)
        for d in list(range(1, n_narrow)) + [0]:
            target = lax.rem(narrow + d, n_narrow)
            group = color * n_narrow + target
            for cut in range(cuts):
                total = None
                for k in range(cut * pairs // cuts, (cut + 1) * pairs // cuts):
                    spot = group * kd + 2 * k
                    rhs = jnp.concatenate([vb[h, index[spot]], vb[h, index[spot + 1]]], axis=0)
                    term = jnp.dot(ta[group, k], rhs, preferred_element_type=jnp.float32)
                    total = term if total is None else total + term
                if cut == 0:
                    acc[...] = fold(total)
                else:
                    acc[...] += fold(total)
                if cut == cuts - 1:
                    if d > 0:
                        psend[s - 1, h, d - 1] = acc[...]
                        part_copy(s - 1, h, d).start()
                    else:
                        own_sum[...] = acc[...]
        step()
        summed = own_sum[...]
        for d in range(1, n_narrow):
            part_copy(s - 1, h, d).wait_recv()
            summed = summed + precv[s - 1, h, d - 1]
        x = solve(s, h, side_ref[pick(color, narrow), :, columns_of(h)] - summed)
        xout[color, :, columns_of(h)] = x

        @pl.when(s < 4)
        def _():
            gathered[s, h, wide] = x
            start_gather(s, h)

    def both(s, carry):
        def move_one():
            @pl.when(s > 1)
            def _():
                middle(s - 1, 1)

        def move_zero():
            @pl.when(s < 4)
            def _():
                middle(s, 0)

        section(s, 0, move_one)
        section(s, 1, move_zero)
        return carry

    lax.fori_loop(1, 5, both, 0)

    for j in range(3):
        out_ref[j] = xout[colors[(wide * n_narrow + narrow) * 3 + j]]

    @pl.loop(0, 4)
    def _(s):
        for h in range(2):
            @pl.loop(0, chips)
            def _(rel):
                sib_copy(s, h, wide, rel).wait_send()

            @pl.loop(1, chips)
            def _(rel):
                ring_copy(s, h, wide, rel, across).wait_send()

            for d in range(1, n_narrow):
                part_copy(s, h, d).wait_send()


def shards(n_wide, n_narrow, right_side, diag_inverse, off_tiles, tile_columns, colors):
    own, tile, labels = right_side.shape
    rows, kd = off_tiles.shape[:2]
    chips = n_wide // 2
    others = n_narrow - 1
    f32, b16 = jnp.float32, jnp.bfloat16
    dma = pltpu.SemaphoreType.DMA
    vmem = pl.BlockSpec(memory_space=pltpu.VMEM)
    smem = pl.BlockSpec(memory_space=pltpu.SMEM)
    return pl.pallas_call(
        functools.partial(kernel, n_wide, n_narrow),
        out_shape=jax.ShapeDtypeStruct((own, tile, labels), f32),
        in_specs=[smem, smem, vmem, vmem, pl.BlockSpec(memory_space=pl.ANY)],
        out_specs=vmem,
        scratch_shapes=[
            pltpu.VMEM((rows, kd, tile, tile), f32),
            pltpu.VMEM((rows, kd // 2, 2 * tile, 2 * tile), b16),
            pltpu.VMEM((3, 2 * tile, tile), b16),
            pltpu.VMEM((2, 3 * n_wide, tile, 2 * HALF), b16),
            pltpu.VMEM((4, 2, n_wide, tile, HALF), f32),
            pltpu.VMEM((4, 2, others, tile, HALF), f32),
            pltpu.VMEM((4, 2, others, tile, HALF), f32),
            pltpu.VMEM((3, tile, labels), f32),
            pltpu.SMEM((rows * kd,), jnp.int32),
            pltpu.VMEM((tile, HALF), f32),
            pltpu.VMEM((tile, HALF), f32),
            dma((rows,)),
            dma((4, 2, chips)),
            dma((4, 2, chips)),
            dma((4, 2, chips)),
            dma((4, 2, chips)),
            dma((4, 2, others)),
            dma((4, 2, others)),
        ],
        compiler_params=pltpu.CompilerParams(
            collective_id=0, has_side_effects=True, vmem_limit_bytes=63 * 1024 * 1024
        ),
        cost_estimate=pl.CostEstimate(flops=8 * 10**9, bytes_accessed=10**7, transcendentals=0),
    )(colors, tile_columns, right_side, diag_inverse, off_tiles)


def solution(mesh):
    return jax.shard_map(
        functools.partial(shards, mesh.shape["wide"], mesh.shape["narrow"]),
        mesh=mesh,
        in_specs=(
            P(("wide", "narrow"), None, None),
            P(("wide", "narrow"), None, None),
            P("wide", "narrow", None, None),
            P("wide", "narrow"),
            P(),
        ),
        out_specs=P(("wide", "narrow"), None, None),
        check_vma=False,
    )
```

```python
import functools

import jax
import jax.numpy as jnp
from jax import lax
from jax.experimental import pallas as pl
from jax.experimental.pallas import tpu as pltpu
from jax.sharding import PartitionSpec as P

MESH = pl.DeviceIdType.MESH
HALF = 128


def split(value):
    high = value.astype(jnp.bfloat16)
    low = (value - high.astype(jnp.float32)).astype(jnp.bfloat16)
    return high, low


def fold(wide_sum):
    t = wide_sum.shape[0] // 2
    return (wide_sum[:t, :HALF] + wide_sum[:t, HALF:]) + (wide_sum[t:, :HALF] + wide_sum[t:, HALF:])


def kernel(
    n_wide, n_narrow, colors, columns, side_ref, diag_ref, tiles_ref, out_ref,
    stage, ta, da, vb, gathered, psend, precv, xout, index, acc, own_sum,
    load_sem, ring_send, ring_recv, sib_send, sib_recv, part_send, part_recv,
):
    wide = lax.axis_index("wide")
    narrow = lax.axis_index("narrow")
    rows, kd = stage.shape[0], stage.shape[1]
    pairs = kd // 2
    chips = n_wide // 2
    zs = chips // 2
    chip, core = lax.div(wide, 2), lax.rem(wide, 2)
    z, y = lax.div(chip, 2), lax.rem(chip, 2)

    def at(at_z, at_y, which):
        return (lax.rem(at_z + zs, zs) * 2 + at_y) * 2 + which

    across, sibling = at(z, 1 - y, core), at(z, y, 1 - core)
    steps = sorted(range(1, zs), key=lambda d: min(d, zs - d))

    for r in range(rows):
        pltpu.make_async_copy(tiles_ref.at[r], stage.at[r], load_sem.at[r]).start()

    for h in range(2):
        @pl.loop(0, 3 * n_wide)
        def _(i):
            vb[h, i] = jnp.zeros(vb.shape[2:], jnp.bfloat16)

    def pick(color, owner_narrow):
        base = (wide * n_narrow + owner_narrow) * 3
        return jnp.where(colors[base + 1] == color, 1, jnp.where(colors[base + 2] == color, 2, 0))

    barrier = pltpu.get_barrier_semaphore()
    for peer in [across, sibling] + [at(z + d, y, core) for d in steps]:
        pl.semaphore_signal(barrier, inc=1, device_id=(peer, narrow), device_id_type=MESH)
    for d in range(1, n_narrow):
        peer = lax.rem(narrow + d, n_narrow)
        pl.semaphore_signal(barrier, inc=1, device_id=(wide, peer), device_id_type=MESH)
    pl.semaphore_wait(barrier, 1 + zs + n_narrow - 1)

    def ring_copy(s, h, origin, rel, target):
        ref = gathered.at[s, h, origin]
        return pltpu.make_async_remote_copy(
            src_ref=ref, dst_ref=ref, send_sem=ring_send.at[s, h, rel], recv_sem=ring_recv.at[s, h, rel],
            device_id=(target, narrow), device_id_type=MESH,
        )

    def sib_copy(s, h, origin, rel):
        ref = gathered.at[s, h, origin]
        return pltpu.make_async_remote_copy(
            src_ref=ref, dst_ref=ref, send_sem=sib_send.at[s, h, rel], recv_sem=sib_recv.at[s, h, rel],
            device_id=(sibling, narrow), device_id_type=MESH,
        )

    def part_copy(s, h, d):
        target = lax.rem(narrow + d, n_narrow)
        return pltpu.make_async_remote_copy(
            src_ref=psend.at[s, h, d - 1], dst_ref=precv.at[s, h, d - 1],
            send_sem=part_send.at[s, h, d - 1], recv_sem=part_recv.at[s, h, d - 1],
            device_id=(wide, target), device_id_type=MESH,
        )

    def color_of(s):
        return s - 2 * jnp.maximum(s - 2, 0)

    def keep(s, h, origin):
        high, low = split(gathered[s, h, origin])
        spot = color_of(s) * n_wide + origin
        vb[h, spot, :, 0:HALF] = high
        vb[h, spot, :, HALF:] = low

    def start_gather(s, h):
        ring_copy(s, h, wide, zs, across).start()
        for d in steps:
            ring_copy(s, h, wide, d, at(z + d, y, core)).start()
        sib_copy(s, h, wide, 0).start()
        keep(s, h, wide)

    def middle(s, h):
        for d in steps:
            origin = at(z - d, y, core)
            ring_copy(s, h, origin, d, across).wait_recv()
            ring_copy(s, h, origin, zs + d, across).start()
            sib_copy(s, h, origin, d).start()
        for d in steps:
            keep(s, h, at(z - d, y, core))

    def finish(s, h):
        for d in [0] + steps:
            origin = at(z - d, 1 - y, core)
            ring_copy(s, h, origin, zs + d, across).wait_recv()
            sib_copy(s, h, origin, zs + d).start()
            keep(s, h, origin)
        for column in range(2):
            for d in [0] + steps:
                origin = at(z - d, y + column * (1 - 2 * y), 1 - core)
                sib_copy(s, h, origin, column * zs + d).wait_recv()
                keep(s, h, origin)

    def solve(s, h, side):
        color = color_of(s)
        high, low = split(side)
        rhs = jnp.concatenate([high, low], axis=1)
        return fold(jnp.dot(da[color], rhs, preferred_element_type=jnp.float32))

    def columns_of(h):
        return slice(h * HALF, (h + 1) * HALF)

    for color in range(3):
        high, low = split(diag_ref[pick(color, narrow)])
        t = high.shape[0]
        da[color, 0:t] = high
        da[color, t:] = low

    for h in range(2):
        gathered[0, h, wide] = solve(0, h, side_ref[pick(0, narrow), :, columns_of(h)])
        start_gather(0, h)

    for color in range(3):
        @pl.loop(0, n_narrow)
        def _(n):
            row = n * 3 + pick(color, n)

            @pl.loop(0, kd)
            def _(k):
                column = columns[row, k]
                index[(color * n_narrow + n) * kd + k] = colors[column] * n_wide + lax.div(column, 3 * n_narrow)

    for r in range(rows):
        pltpu.make_async_copy(tiles_ref.at[r], stage.at[r], load_sem.at[r]).wait()

    for turn, color in enumerate((1, 2, 0)):
        @pl.loop(0, n_narrow)
        def _(n):
            row = n * 3 + pick(color, n)
            t = stage.shape[2]

            @pl.loop(0, kd // 2)
            def _(k):
                for part in range(2):
                    high, low = split(stage[row, 2 * k + part])
                    ta[color * n_narrow + n, k, 0:t, part * t:(part + 1) * t] = high
                    ta[color * n_narrow + n, k, t:, part * t:(part + 1) * t] = low

        if turn < 2:
            middle(0, turn)

    cuts = 2 if pairs % 2 == 0 else 1

    def section(s, h, step):
        color = color_of(s)
        finish(s - 1, h)
        for d in list(range(1, n_narrow)) + [0]:
            target = lax.rem(narrow + d, n_narrow)
            group = color * n_narrow + target
            for cut in range(cuts):
                total = None
                for k in range(cut * pairs // cuts, (cut + 1) * pairs // cuts):
                    spot = group * kd + 2 * k
                    rhs = jnp.concatenate([vb[h, index[spot]], vb[h, index[spot + 1]]], axis=0)
                    term = jnp.dot(ta[group, k], rhs, preferred_element_type=jnp.float32)
                    total = term if total is None else total + term
                if cut == 0:
                    acc[...] = fold(total)
                else:
                    acc[...] += fold(total)
                if cut == cuts - 1:
                    if d > 0:
                        psend[s - 1, h, d - 1] = acc[...]
                        part_copy(s - 1, h, d).start()
                        if d == n_narrow - 1:
                            step()
                    else:
                        own_sum[...] = acc[...]
        summed = own_sum[...]
        for d in range(1, n_narrow):
            part_copy(s - 1, h, d).wait_recv()
            summed = summed + precv[s - 1, h, d - 1]
        x = solve(s, h, side_ref[pick(color, narrow), :, columns_of(h)] - summed)
        xout[color, :, columns_of(h)] = x

        @pl.when(s < 4)
        def _():
            gathered[s, h, wide] = x
            start_gather(s, h)

    def both(s, carry):
        def move_one():
            @pl.when(s > 1)
            def _():
                middle(s - 1, 1)

        def move_zero():
            @pl.when(s < 4)
            def _():
                middle(s, 0)

        section(s, 0, move_one)
        section(s, 1, move_zero)
        return carry

    lax.fori_loop(1, 5, both, 0)

    for j in range(3):
        out_ref[j] = xout[colors[(wide * n_narrow + narrow) * 3 + j]]

    @pl.loop(0, 4)
    def _(s):
        for h in range(2):
            @pl.loop(0, chips)
            def _(rel):
                sib_copy(s, h, wide, rel).wait_send()

            @pl.loop(1, chips)
            def _(rel):
                ring_copy(s, h, wide, rel, across).wait_send()

            for d in range(1, n_narrow):
                part_copy(s, h, d).wait_send()


def shards(n_wide, n_narrow, right_side, diag_inverse, off_tiles, tile_columns, colors):
    own, tile, labels = right_side.shape
    rows, kd = off_tiles.shape[:2]
    chips = n_wide // 2
    others = n_narrow - 1
    f32, b16 = jnp.float32, jnp.bfloat16
    dma = pltpu.SemaphoreType.DMA
    vmem = pl.BlockSpec(memory_space=pltpu.VMEM)
    smem = pl.BlockSpec(memory_space=pltpu.SMEM)
    return pl.pallas_call(
        functools.partial(kernel, n_wide, n_narrow),
        out_shape=jax.ShapeDtypeStruct((own, tile, labels), f32),
        in_specs=[smem, smem, vmem, vmem, pl.BlockSpec(memory_space=pl.ANY)],
        out_specs=vmem,
        scratch_shapes=[
            pltpu.VMEM((rows, kd, tile, tile), f32),
            pltpu.VMEM((rows, kd // 2, 2 * tile, 2 * tile), b16),
            pltpu.VMEM((3, 2 * tile, tile), b16),
            pltpu.VMEM((2, 3 * n_wide, tile, 2 * HALF), b16),
            pltpu.VMEM((4, 2, n_wide, tile, HALF), f32),
            pltpu.VMEM((4, 2, others, tile, HALF), f32),
            pltpu.VMEM((4, 2, others, tile, HALF), f32),
            pltpu.VMEM((3, tile, labels), f32),
            pltpu.SMEM((rows * kd,), jnp.int32),
            pltpu.VMEM((tile, HALF), f32),
            pltpu.VMEM((tile, HALF), f32),
            dma((rows,)),
            dma((4, 2, chips)),
            dma((4, 2, chips)),
            dma((4, 2, chips)),
            dma((4, 2, chips)),
            dma((4, 2, others)),
            dma((4, 2, others)),
        ],
        compiler_params=pltpu.CompilerParams(
            collective_id=0, has_side_effects=True, vmem_limit_bytes=63 * 1024 * 1024
        ),
        cost_estimate=pl.CostEstimate(flops=8 * 10**9, bytes_accessed=10**7, transcendentals=0),
    )(colors, tile_columns, right_side, diag_inverse, off_tiles)


def solution(mesh):
    return jax.shard_map(
        functools.partial(shards, mesh.shape["wide"], mesh.shape["narrow"]),
        mesh=mesh,
        in_specs=(
            P(("wide", "narrow"), None, None),
            P(("wide", "narrow"), None, None),
            P("wide", "narrow", None, None),
            P("wide", "narrow"),
            P(),
        ),
        out_specs=P(("wide", "narrow"), None, None),
        check_vma=False,
    )
```
